128 devices in a mesh: stream: 16 (over z, y), cross: 8 (over x, core).
Axes of the slice: x: 4, y: 4, z: 4, core: 2. Of those that a mesh axis runs over, the one named last changes fastest.
Arguments:
- flow_state: float32 [16, 8, 12, 64, 256], P('stream', 'cross'), may hold values from 0.04 to 7.2, as said below
- flux_blocks: bfloat16 [16, 8, 7, 64, 64, 256], P('stream', 'cross'), may hold values from -0.25 to 0.25
- block_links: int32 [16, 8, 7, 256], P('stream', 'cross'), may hold values from 0 to 255
- face_cells: int32 [16, 8, 4, 1536], P('stream', 'cross'), may hold values from 0 to 16383
- face_weight: float32 [16, 8, 4, 1536], P('stream', 'cross'), may hold values from 0.05 to 0.5
- point_owner: int32 [16, 8, 32768], P('stream', 'cross'), may hold values from 0 to 8, as said below
- point_slot: int32 [16, 8, 32768], P('stream', 'cross'), may hold values from 0 to 127, as said below
- point_block: int32 [16, 8, 32768], P('stream', 'cross'), may hold values from 0 to 255
- point_weight: bfloat16 [16, 8, 64, 32768], P('stream', 'cross'), may hold values from 0 to 0.03125
- point_area: float32 [16, 8, 32768], P('stream', 'cross'), may hold values from 0.1 to 1
- pellet_gain: float32 [16, 8, 9, 128], P('stream', 'cross'), may hold values from 0.3 to 3
Outputs:
- next_state: float32 [16, 8, 12, 64, 256], P('stream', 'cross')
- pellet_rate: float32 [16, 8, 9, 128], P('stream', 'cross')
The draws below stay inside these ranges and needn't reach their ends.
Inputs may be any that keep to these rules, and one draw needn't show every extreme that they name: `flow_state`: values at every size stay within the range; each tile has its own level per component. `point_owner`: code 3 a + c names the tile at offset (a - 1, c - 1) along stream and cross; it never names a tile outside the bed; the first 128 points of every tile have code 4. `point_slot`: the first 128 points of every tile have slot equal to their position, so every owned pellet has points on its own tile.
All inputs are finite; a program needn't handle non-finite values.
Results may differ from the reference program's by a relative error of at most 0.0003.
The reference program's roundings to bfloat16 on the way (of `rounded` and `spread`) count: a program that leaves them out, or rounds other values in their place, can miss the bound.
Values sent between devices are 32-bit elements; how exact they have to be, the bound alone decides.
A program may use at most 128 MiB of HBM per device.

```python
import math
import jax
import jax.numpy as jnp
from jax import lax

Q = 12
R = 9
B = 64
K = 7
NB = 256
NF = 1536
PEL = 128
PTS = 32768
STREAM_TILES = 16
CROSS_TILES = 8


def draw_flow_state(key, part):
    first_key, second_key = jax.random.split(jax.random.fold_in(key, 11))
    level = jnp.exp(jax.random.uniform(first_key, (STREAM_TILES, CROSS_TILES, Q, 1, 1), jnp.float32, jnp.log(0.3), jnp.log(3.0)))
    rough = jax.random.uniform(second_key, (STREAM_TILES, CROSS_TILES, Q, B, NB), jnp.float32, 0.5, 1.5)
    return level * rough


def draw_point_owner(key, part):
    shape = (STREAM_TILES, CROSS_TILES, PTS)
    pick = jax.random.randint(jax.random.fold_in(key, 23), shape, 0, 16)
    codes = jnp.array([4, 4, 4, 4, 4, 4, 4, 4, 0, 1, 2, 3, 5, 6, 7, 8], jnp.int32)
    code = codes[pick]
    stream_pos = lax.broadcasted_iota(jnp.int32, shape, 0)
    cross_pos = lax.broadcasted_iota(jnp.int32, shape, 1)
    position = lax.broadcasted_iota(jnp.int32, shape, 2)
    stream_step = code // 3 - 1
    cross_step = code % 3 - 1
    outside = (stream_pos + stream_step < 0) | (stream_pos + stream_step >= STREAM_TILES)
    outside = outside | (cross_pos + cross_step < 0) | (cross_pos + cross_step >= CROSS_TILES)
    outside = outside | (position < PEL)
    return jnp.where(outside, 4, code).astype(jnp.int32)


def draw_point_slot(key, part):
    shape = (STREAM_TILES, CROSS_TILES, PTS)
    drawn = jax.random.randint(jax.random.fold_in(key, 37), shape, 0, PEL)
    position = lax.broadcasted_iota(jnp.int32, shape, 2)
    return jnp.where(position < PEL, position, drawn).astype(jnp.int32)


def place_ends(values, key, low, top_value):
    shape = values.shape
    spot = [jax.random.randint(jax.random.fold_in(key, axis), (), 0, shape[axis]) for axis in range(len(shape))]
    values = values.at[tuple(spot)].set(low)
    longest = shape.index(max(shape))
    spot[longest] = (spot[longest] + 1) % shape[longest]
    return values.at[tuple(spot)].set(top_value)


def block_levels(key, shape, cuts, least, high):
    level, own = 1.0, jax.random.fold_in(key, 6)
    for dim, blocks in cuts:
        steps = jnp.exp(jax.random.uniform(jax.random.fold_in(own, dim), (blocks,), jnp.float32, least / len(cuts), high / len(cuts)))
        level = level * jnp.repeat(steps, shape[dim] // blocks).reshape([-1 if axis == dim else 1 for axis in range(len(shape))])
    return level


def centred(own_key, dims, scale, limit, shards=(), dtype=jnp.bfloat16):
    factor_of = block_levels(own_key, dims, shards, -0.22, 0.18) if shards else 1.0
    values = jax.random.normal(own_key, dims, jnp.float32) * scale * factor_of
    return jnp.minimum(jnp.maximum(values, -limit), limit).astype(dtype)


def setup_inputs(seed: int = 0) -> dict:
    key_list = jax.random.split(jax.random.key(seed), 12)
    flow_state = draw_flow_state(jax.random.fold_in(key_list[11], 71), 0)
    flux_blocks = centred(key_list[1], (STREAM_TILES, CROSS_TILES, K, B, B, NB), (B * K) ** -0.5, 0.25, ((0, 16), (1, 8)))
    block_links = place_ends(jax.random.randint(key_list[2], (STREAM_TILES, CROSS_TILES, K, NB), 0, NB), jax.random.fold_in(key_list[2], 1), 0, NB - 1).astype(jnp.int32)
    face_cells = place_ends(jax.random.randint(key_list[3], (STREAM_TILES, CROSS_TILES, 4, NF), 0, B * NB), jax.random.fold_in(key_list[3], 1), 0, (B * NB) - 1).astype(jnp.int32)
    face_weight = jnp.clip(jnp.exp(math.log(0.5) - 2.3025851 * jax.random.uniform(key_list[4], (STREAM_TILES, CROSS_TILES, 4, NF), jnp.float32) ** block_levels(key_list[4], (STREAM_TILES, CROSS_TILES, 4, NF), ((0, 16), (1, 8)), -0.2, 0.2)), 0.05, 0.5)
    point_owner = draw_point_owner(jax.random.fold_in(key_list[11], 71), 0)
    point_slot = draw_point_slot(jax.random.fold_in(key_list[11], 71), 0)
    point_block = place_ends(jax.random.randint(key_list[7], (STREAM_TILES, CROSS_TILES, PTS), 0, NB), jax.random.fold_in(key_list[7], 1), 0, NB - 1).astype(jnp.int32)
    point_weight = jnp.clip(0.03125 * jax.random.uniform(key_list[8], (STREAM_TILES, CROSS_TILES, B, PTS), jnp.float32) ** block_levels(key_list[8], (STREAM_TILES, CROSS_TILES, B, PTS), ((0, 16), (1, 8)), -0.2, 0.2), 0.0, 0.03125).astype(jnp.bfloat16)
    point_area = jnp.clip(jnp.exp(math.log(1.0) - 2.3025851 * jax.random.uniform(key_list[9], (STREAM_TILES, CROSS_TILES, PTS), jnp.float32) ** block_levels(key_list[9], (STREAM_TILES, CROSS_TILES, PTS), ((0, 16), (1, 8)), -0.2, 0.2)), 0.1, 1.0)
    pellet_gain = jnp.clip(jnp.exp(math.log(3.0) - 2.3025851 * jax.random.uniform(key_list[10], (STREAM_TILES, CROSS_TILES, R, PEL), jnp.float32) ** block_levels(key_list[10], (STREAM_TILES, CROSS_TILES, R, PEL), ((0, 16), (1, 8)), -0.2, 0.2)), 0.3, 3.0)
    return {"flow_state": flow_state, "flux_blocks": flux_blocks, "block_links": block_links, "face_cells": face_cells, "face_weight": face_weight, "point_owner": point_owner, "point_slot": point_slot, "point_block": point_block, "point_weight": point_weight, "point_area": point_area, "pellet_gain": pellet_gain}


phase_dt = 0.5

def tile_local(args):
    state, matrices, links, cell_ids, face_gain, owner, slot, block_ids, interp, area = args
    rounded = lax.optimization_barrier(state.astype(jnp.bfloat16))
    gathered = rounded[:, :, links].astype(jnp.float32)
    interior = jnp.einsum('kijb,qjkb->qib', matrices.astype(jnp.float32), gathered)
    flat = state.reshape(Q, B * NB)
    outgoing = face_gain[:, None, :] * jnp.transpose(flat[:, cell_ids], (1, 0, 2))
    picked = rounded[:R][:, :, block_ids].astype(jnp.float32)
    values = lax.optimization_barrier(jnp.sum(picked * interp.astype(jnp.float32)[None], axis=1))
    stacked = jnp.concatenate([values * area[None], area[None]], axis=0)
    bins = owner * PEL + slot
    partial_value = jax.ops.segment_sum(stacked.T, bins, num_segments=9 * PEL)
    partial_value = partial_value.reshape(3, 3, PEL, R + 1).transpose(0, 1, 3, 2)
    return (interior, outgoing, partial_value)

def tile_finish(args):
    state, interior, cell_ids, net, owner, slot, block_ids, interp, area, neighbour_rates = args
    face_term = jnp.zeros((Q, B * NB), jnp.float32).at[:, cell_ids.reshape(-1)].add(jnp.transpose(net, (1, 0, 2)).reshape(Q, -1))
    lookup = neighbour_rates.reshape(9, R, PEL).transpose(1, 0, 2).reshape(R, 9 * PEL)
    source = area[None] * lookup[:, owner * PEL + slot]
    spread = (interp.astype(jnp.float32)[None] * source[:, None, :]).astype(jnp.bfloat16)
    spread = lax.optimization_barrier(spread)
    surface = jax.ops.segment_sum(spread.astype(jnp.float32).transpose(2, 0, 1), block_ids, num_segments=NB).transpose(1, 2, 0)
    whole = jnp.concatenate([surface, jnp.zeros((Q - R, B, NB), jnp.float32)], axis=0)
    return state + phase_dt * (interior + face_term.reshape(Q, B, NB) + whole)

def reference(flow_state, flux_blocks, block_links, face_cells, face_weight, point_owner, point_slot, point_block, point_weight, point_area, pellet_gain):
    tiles = STREAM_TILES * CROSS_TILES

    def flatten(array):
        return array.reshape((tiles,) + array.shape[2:])
    local_in = tuple((flatten(a) for a in (flow_state, flux_blocks, block_links, face_cells, face_weight, point_owner, point_slot, point_block, point_weight, point_area)))
    interior, outgoing, partial_value = lax.map(tile_local, local_in)
    outgoing = outgoing.reshape((STREAM_TILES, CROSS_TILES) + outgoing.shape[1:])
    partial_value = partial_value.reshape((STREAM_TILES, CROSS_TILES) + partial_value.shape[1:])
    zero_row = jnp.zeros((1, CROSS_TILES, Q, NF), jnp.float32)
    zero_col = jnp.zeros((STREAM_TILES, 1, Q, NF), jnp.float32)
    from_lower = jnp.concatenate([zero_row, outgoing[:-1, :, 1]], axis=0)
    from_upper = jnp.concatenate([outgoing[1:, :, 0], zero_row], axis=0)
    from_left = jnp.concatenate([zero_col, outgoing[:, :-1, 3]], axis=1)
    from_right = jnp.concatenate([outgoing[:, 1:, 2], zero_col], axis=1)
    incoming = jnp.stack([from_lower, from_upper, from_left, from_right], axis=2)
    net = incoming - outgoing
    padded = jnp.pad(partial_value, ((1, 1), (1, 1), (0, 0), (0, 0), (0, 0), (0, 0)))
    totals = jnp.zeros((STREAM_TILES, CROSS_TILES, R + 1, PEL), jnp.float32)
    for first in range(3):
        for second in range(3):
            totals = totals + padded[2 - first:2 - first + STREAM_TILES, 2 - second:2 - second + CROSS_TILES, first, second]
    mean = totals[:, :, :R] / totals[:, :, R:R + 1]
    pellet_rate = pellet_gain * mean / jnp.sqrt(1.0 + mean * mean)
    rate_pad = jnp.pad(pellet_rate, ((1, 1), (1, 1), (0, 0), (0, 0)))
    rows_of = []
    for first in range(3):
        cols_of = []
        for second in range(3):
            cols_of.append(rate_pad[first:first + STREAM_TILES, second:second + CROSS_TILES])
        rows_of.append(jnp.stack(cols_of, axis=2))
    neighbour_rates = jnp.stack(rows_of, axis=2)
    finish_in = (flatten(flow_state), interior, flatten(face_cells), flatten(net), flatten(point_owner), flatten(point_slot), flatten(point_block), flatten(point_weight), flatten(point_area), flatten(neighbour_rates))
    next_state = lax.map(tile_finish, finish_in)
    next_state = next_state.reshape(flow_state.shape)
    return (next_state, pellet_rate)
```

```python
import functools

import jax
import jax.numpy as jnp
from jax import lax
from jax.experimental import pallas as pl
from jax.experimental.pallas import tpu as pltpu
from jax.sharding import PartitionSpec as P

R = 9
PEL = 128
GROUP = 16
POINT_STEP = 2048
FACE_STEP = 1536
OWNER_PAIRS = 5
ROWS = 16

phase_dt = 0.5
f32 = jnp.float32
bf16 = jnp.bfloat16
OFFSETS = [(a, c) for a in range(3) for c in range(3)]
AROUND = [n for n in range(9) if n != 4]


def one_hot(row, count):
    ids = row.astype(f32).astype(bf16)
    iota = lax.broadcasted_iota(jnp.int32, (count, row.shape[1]), 0).astype(f32).astype(bf16)
    return jnp.where(iota == ids, bf16(1), bf16(0))


def split(values):
    high = values.astype(bf16)
    return high, (values - high.astype(f32)).astype(bf16)


def dot(a, b):
    return jnp.dot(a, b, preferred_element_type=f32)


def dot_t(a, b):
    return lax.dot_general(a, b, (((1,), (1,)), ((), ())), preferred_element_type=f32)


def kernel(
    stream_count,
    cross_count,
    state_hbm, flux_hbm, links_hbm, cells_hbm, face_gain_hbm, owner_hbm, slot_hbm, block_hbm,
    weight_hbm, area_hbm, gain_hbm,
    next_ref, rates_ref,
    state_ref, flux_ref, links_ref, cells_ref, face_gain_ref, owner_ref, slot_ref, block_ref,
    weight_ref, area_ref, gain_ref,
    split_ref, coupled_ref, grouped_ref, total_ref,
    face_out, face_in, part_out, part_in, rate_out, rate_in, binned_ref, table_ref,
    in_sem, face_send, face_recv, part_send, part_recv, rate_send, rate_recv,
):
    s, x = lax.axis_index("stream"), lax.axis_index("cross")
    components, cell_rows, blocks = state_ref.shape
    rows = components * cell_rows
    slots = flux_ref.shape[0]
    points = block_ref.shape[1]
    faces = face_gain_ref.shape[1] // 4

    def at(first, second):
        return (
            lax.rem(s + (first + stream_count), stream_count),
            lax.rem(x + (second + cross_count), cross_count),
        )

    pairs = [
        (state_hbm, state_ref), (cells_hbm, cells_ref), (face_gain_hbm, face_gain_ref),
        (block_hbm, block_ref), (owner_hbm, owner_ref), (slot_hbm, slot_ref), (area_hbm, area_ref),
        (weight_hbm, weight_ref), (links_hbm, links_ref), (gain_hbm, gain_ref), (flux_hbm, flux_ref),
    ]
    loads = [pltpu.make_async_copy(a, b, in_sem.at[n]) for n, (a, b) in enumerate(pairs)]
    for load in loads:
        load.start()
    barrier = pltpu.get_barrier_semaphore()
    for n in AROUND:
        a, c = OFFSETS[n]
        pl.semaphore_signal(
            barrier, inc=1, device_id=at(a - 1, c - 1), device_id_type=pl.DeviceIdType.MESH
        )

    for load in loads[:3]:
        load.wait()
    high, low = split(state_ref[...].reshape(rows, blocks))
    split_ref[0:rows] = high
    split_ref[rows:2 * rows] = low
    cell_iota = lax.broadcasted_iota(jnp.int32, (cell_rows, FACE_STEP), 0)

    def gather_faces(side, carry):
        first = pl.multiple_of(side * faces, 128)
        ids = cells_ref[0:1, pl.ds(first, FACE_STEP)]
        table = one_hot(ids % blocks, blocks)
        both = dot(split_ref[...], table)
        chosen = both[:rows] + both[rows:]
        here = jnp.where((ids // blocks == cell_iota)[None], chosen.reshape(components, cell_rows, -1), 0.0)
        gain = face_gain_ref[0:1, pl.ds(first, FACE_STEP)]
        face_out[side, 0:components] = jnp.sum(here, axis=1) * gain
        face_out[side, components:ROWS] = jnp.zeros((ROWS - components, FACE_STEP), f32)
        return carry

    lax.fori_loop(0, 4, gather_faces, 0)
    pl.semaphore_wait(barrier, len(AROUND))
    sides = [(-1, 0, 1), (1, 0, 0), (0, -1, 3), (0, 1, 2)]
    face_copies = [
        pltpu.make_async_remote_copy(
            src_ref=face_out.at[d],
            dst_ref=face_in.at[opposite],
            send_sem=face_send.at[d],
            recv_sem=face_recv.at[opposite],
            device_id=at(da, dc),
            device_id_type=pl.DeviceIdType.MESH,
        )
        for d, (da, dc, opposite) in enumerate(sides)
    ]
    for copy in face_copies:
        copy.start()

    for load in loads[3:8]:
        load.wait()
    binned_ref[...] = jnp.zeros_like(binned_ref)

    def pellet_code(first):
        owner = owner_ref[0:1, pl.ds(first, POINT_STEP)]
        slot = slot_ref[0:1, pl.ds(first, POINT_STEP)]
        return owner // 2, one_hot((owner % 2) * PEL + slot, 2 * PEL)

    def interpolate(step, carry):
        first = pl.multiple_of(step * POINT_STEP, POINT_STEP)
        table = one_hot(block_ref[0:1, pl.ds(first, POINT_STEP)], blocks)
        picked = dot(split_ref[0:R * cell_rows], table).reshape(R, cell_rows, POINT_STEP)
        weights = weight_ref[:, pl.ds(first, POINT_STEP)].astype(f32)
        values = jnp.sum(picked * weights[None], axis=1)
        area = area_ref[0:1, pl.ds(first, POINT_STEP)]
        stacked = jnp.concatenate(
            [values * area, area, jnp.zeros((ROWS - R - 1, POINT_STEP), f32)], axis=0
        )
        high, low = split(stacked)
        pair, pellets = pellet_code(first)
        both = jnp.concatenate([high.astype(f32), low.astype(f32)], axis=0)
        masked = jnp.concatenate([jnp.where(pair == g, both, 0.0) for g in range(OWNER_PAIRS)], axis=0)
        binned_ref[...] += dot_t(masked.astype(bf16), pellets)
        return carry

    lax.fori_loop(0, points // POINT_STEP, interpolate, 0)
    for n in range(9):
        first = (n // 2) * 2 * ROWS
        lanes = slice((n % 2) * PEL, (n % 2 + 1) * PEL)
        part_out[n] = (
            binned_ref[first:first + ROWS, lanes] + binned_ref[first + ROWS:first + 2 * ROWS, lanes]
        )
    part_copies = [
        pltpu.make_async_remote_copy(
            src_ref=part_out.at[n],
            dst_ref=part_in.at[n],
            send_sem=part_send.at[n],
            recv_sem=part_recv.at[n],
            device_id=at(OFFSETS[n][0] - 1, OFFSETS[n][1] - 1),
            device_id_type=pl.DeviceIdType.MESH,
        )
        for n in AROUND
    ]
    for copy in part_copies:
        copy.start()

    for load in loads[8:]:
        load.wait()
    groups = blocks // GROUP
    width = components * GROUP

    for k in range(slots):
        table = one_hot(links_ref[k:k + 1, :], blocks)
        coupled = dot(split_ref[0:rows], table).astype(bf16).reshape(components, cell_rows, blocks)
        for g in range(groups):
            lanes = slice(g * GROUP, (g + 1) * GROUP)
            coupled_ref[g, k * cell_rows:(k + 1) * cell_rows, 0:width] = jnp.concatenate(
                [coupled[q, :, lanes] for q in range(components)], axis=1
            )

    step = 8
    mask = (
        lax.broadcasted_iota(jnp.int32, (1, GROUP, width), 2) % GROUP
        == lax.broadcasted_iota(jnp.int32, (1, GROUP, width), 1)
    )

    def couple(which, carry):
        first = pl.multiple_of(which * step, step)
        turned = [
            jnp.transpose(flux_ref[:, first + n].reshape(slots * cell_rows, blocks)) for n in range(step)
        ]
        for g in range(groups):
            left = jnp.concatenate([t[g * GROUP:(g + 1) * GROUP] for t in turned], axis=0)
            product = dot(left, coupled_ref[g, :, 0:width]).reshape(step, GROUP, width)
            grouped_ref[g, pl.ds(first, step), 0:width] = jnp.sum(jnp.where(mask, product, 0.0), axis=1)
        return carry

    lax.fori_loop(0, cell_rows // step, couple, 0)

    totals = part_out[4]
    for copy in part_copies:
        copy.wait()
    for n in AROUND:
        totals = totals + part_in[n]
    mean = totals[0:R] / totals[R:R + 1]
    rates = gain_ref[...] * mean / jnp.sqrt(1.0 + mean * mean)
    rates_ref[...] = rates
    rate_out[0:R] = rates
    rate_out[R:ROWS] = jnp.zeros((ROWS - R, PEL), f32)
    rate_copies = [
        pltpu.make_async_remote_copy(
            src_ref=rate_out,
            dst_ref=rate_in.at[n],
            send_sem=rate_send.at[n],
            recv_sem=rate_recv.at[n],
            device_id=at(1 - OFFSETS[n][0], 1 - OFFSETS[n][1]),
            device_id_type=pl.DeviceIdType.MESH,
        )
        for n in AROUND
    ]
    for copy in rate_copies:
        copy.start()

    for q in range(components):
        total_ref[q * cell_rows:(q + 1) * cell_rows] = jnp.concatenate(
            [grouped_ref[g, :, q * GROUP:(q + 1) * GROUP] for g in range(groups)], axis=1
        )
    for copy in face_copies:
        copy.wait()
    inside = [s > 0, s < stream_count - 1, x > 0, x < cross_count - 1]
    present = [jnp.where(here, 1.0, 0.0) for here in inside]
    for d in range(4):
        face_in[d] = face_in[d] * present[d] - face_out[d]

    def add_faces(side, carry):
        first = pl.multiple_of(side * faces, 128)
        ids = cells_ref[0:1, pl.ds(first, FACE_STEP)]
        table = one_hot(ids % blocks, blocks)
        here = ids // blocks == cell_iota
        net = face_in[side, 0:components]
        spread = jnp.where(here[None], net[:, None, :], 0.0).reshape(rows, FACE_STEP)
        high, low = split(spread)
        total_ref[...] += dot_t(high, table) + dot_t(low, table)
        return carry

    lax.fori_loop(0, 4, add_faces, 0)

    rate_in[4] = rate_out[...]
    for copy in rate_copies:
        copy.wait()
    for n in range(9):
        first = (n // 2) * 2 * ROWS
        lanes = slice((n % 2) * PEL, (n % 2 + 1) * PEL)
        high, low = split(rate_in[n])
        table_ref[first:first + ROWS, lanes] = high
        table_ref[first + ROWS:first + 2 * ROWS, lanes] = low
    table_ref[8 * ROWS:10 * ROWS, PEL:2 * PEL] = jnp.zeros((2 * ROWS, PEL), bf16)

    def deposit(step, carry):
        first = pl.multiple_of(step * POINT_STEP, POINT_STEP)
        pair, pellets = pellet_code(first)
        found = dot(table_ref[...], pellets)
        source = jnp.zeros((ROWS, POINT_STEP), f32)
        for g in range(OWNER_PAIRS):
            top = g * 2 * ROWS
            rate = found[top:top + ROWS] + found[top + ROWS:top + 2 * ROWS]
            source = jnp.where(pair == g, rate, source)
        source = source * area_ref[0:1, pl.ds(first, POINT_STEP)]
        table = one_hot(block_ref[0:1, pl.ds(first, POINT_STEP)], blocks)
        weights = weight_ref[:, pl.ds(first, POINT_STEP)].astype(f32)
        spread = (weights[None] * source[0:R, None, :]).astype(bf16).reshape(R * cell_rows, POINT_STEP)
        total_ref[0:R * cell_rows] += dot_t(spread, table)
        return carry

    lax.fori_loop(0, points // POINT_STEP, deposit, 0)
    next_ref[...] = state_ref[...] + phase_dt * total_ref[...].reshape(components, cell_rows, blocks)


def shards(mesh_shape, *arrays):
    arrays = [array[0, 0] for array in arrays]
    (state, flux, links, cells, face_gain, owner, slot, block, weight, area, gain) = arrays
    components, cell_rows, blocks = state.shape
    slots = flux.shape[0]
    rows = components * cell_rows
    cells = cells.reshape(1, -1)
    face_gain = face_gain.reshape(1, -1)
    owner, slot, block, area = (a.reshape(1, -1) for a in (owner, slot, block, area))
    operands = (state, flux, links, cells, face_gain, owner, slot, block, weight, area, gain)
    faces = cells.shape[1] // 4
    groups = blocks // GROUP
    dma = pltpu.SemaphoreType.DMA
    result, rates = pl.pallas_call(
        functools.partial(kernel, *mesh_shape),
        out_shape=(
            jax.ShapeDtypeStruct(state.shape, f32),
            jax.ShapeDtypeStruct(gain.shape, f32),
        ),
        in_specs=[pl.BlockSpec(memory_space=pl.ANY)] * len(operands),
        out_specs=(pl.BlockSpec(memory_space=pltpu.VMEM),) * 2,
        scratch_shapes=[pltpu.VMEM(a.shape, a.dtype) for a in operands]
        + [
            pltpu.VMEM((2 * rows, blocks), bf16),
            pltpu.VMEM((groups, slots * cell_rows, 256), bf16),
            pltpu.VMEM((groups, cell_rows, 256), f32),
            pltpu.VMEM((rows, blocks), f32),
            pltpu.VMEM((4, ROWS, faces), f32),
            pltpu.VMEM((4, ROWS, faces), f32),
            pltpu.VMEM((9, ROWS, PEL), f32),
            pltpu.VMEM((9, ROWS, PEL), f32),
            pltpu.VMEM((ROWS, PEL), f32),
            pltpu.VMEM((9, ROWS, PEL), f32),
            pltpu.VMEM((OWNER_PAIRS * 2 * ROWS, 2 * PEL), f32),
            pltpu.VMEM((OWNER_PAIRS * 2 * ROWS, 2 * PEL), bf16),
            dma((len(operands),)),
            dma((4,)),
            dma((4,)),
            dma((9,)),
            dma((9,)),
            dma((9,)),
            dma((9,)),
        ],
        compiler_params=pltpu.CompilerParams(
            collective_id=0, has_side_effects=True, vmem_limit_bytes=60 * 2**20
        ),
        name="bed_phase",
    )(*operands)
    return result[None, None], rates[None, None]


def solution(mesh):
    def spec(dims):
        return P("stream", "cross", *([None] * dims))

    return jax.shard_map(
        functools.partial(shards, (mesh.shape["stream"], mesh.shape["cross"])),
        mesh=mesh,
        in_specs=tuple(spec(d) for d in (3, 4, 2, 2, 2, 1, 1, 1, 2, 1, 2)),
        out_specs=(spec(3), spec(2)),
        check_vma=False,
    )
```

```python
import functools

import jax
import jax.numpy as jnp
from jax import lax
from jax.experimental import pallas as pl
from jax.experimental.pallas import tpu as pltpu
from jax.sharding import PartitionSpec as P

R = 9
PEL = 128
GROUP = 16
POINT_STEP = 4096
FACE_STEP = 1536
OWNER_PAIRS = 5
ROWS = 16

phase_dt = 0.5
f32 = jnp.float32
bf16 = jnp.bfloat16
OFFSETS = [(a, c) for a in range(3) for c in range(3)]
AROUND = [n for n in range(9) if n != 4]


def one_hot(row, count):
    ids = row.astype(f32).astype(bf16)
    iota = lax.broadcasted_iota(jnp.int32, (count, row.shape[1]), 0).astype(f32).astype(bf16)
    return jnp.where(iota == ids, bf16(1), bf16(0))


def split(values):
    high = values.astype(bf16)
    return high, (values - high.astype(f32)).astype(bf16)


def dot(a, b):
    return jnp.dot(a, b, preferred_element_type=f32)


def dot_t(a, b):
    return lax.dot_general(a, b, (((1,), (1,)), ((), ())), preferred_element_type=f32)


def kernel(
    stream_count,
    cross_count,
    state_hbm, flux_hbm, links_hbm, cells_hbm, face_gain_hbm, owner_hbm, slot_hbm, block_hbm,
    weight_hbm, area_hbm, gain_hbm,
    next_ref, rates_ref,
    state_ref, flux_ref, links_ref, cells_ref, face_gain_ref, owner_ref, slot_ref, block_ref,
    weight_ref, area_ref, gain_ref,
    split_ref, coupled_ref, grouped_ref, total_ref,
    face_out, face_in, part_out, part_in, rate_out, rate_in, binned_ref, last_ref, source_ref,
    in_sem, face_send, face_recv, part_send, part_recv, rate_send, rate_recv,
):
    s, x = lax.axis_index("stream"), lax.axis_index("cross")
    components, cell_rows, blocks = state_ref.shape
    rows = components * cell_rows
    slots = flux_ref.shape[0]
    points = block_ref.shape[1]
    faces = face_gain_ref.shape[1]

    def at(first, second):
        return (
            lax.rem(s + (first + stream_count), stream_count),
            lax.rem(x + (second + cross_count), cross_count),
        )

    pairs = [
        (state_hbm, state_ref), (cells_hbm, cells_ref), (face_gain_hbm, face_gain_ref),
        (block_hbm, block_ref), (owner_hbm, owner_ref), (slot_hbm, slot_ref), (area_hbm, area_ref),
        (weight_hbm, weight_ref), (links_hbm, links_ref), (gain_hbm, gain_ref), (flux_hbm, flux_ref),
    ]
    loads = [pltpu.make_async_copy(a, b, in_sem.at[n]) for n, (a, b) in enumerate(pairs)]
    for load in loads:
        load.start()
    barrier = pltpu.get_barrier_semaphore()
    for n in AROUND:
        a, c = OFFSETS[n]
        pl.semaphore_signal(
            barrier, inc=1, device_id=at(a - 1, c - 1), device_id_type=pl.DeviceIdType.MESH
        )

    for load in loads[:3]:
        load.wait()
    high, low = split(state_ref[...].reshape(rows, blocks))
    split_ref[0:rows] = high
    split_ref[rows:2 * rows] = low
    cell_iota = lax.broadcasted_iota(jnp.int32, (cell_rows, FACE_STEP), 0)

    def gather_faces(side, carry):
        ids = cells_ref[pl.ds(side, 1), :]
        table = one_hot(ids % blocks, blocks)
        both = dot(split_ref[...], table)
        chosen = both[:rows] + both[rows:]
        here = jnp.where((ids // blocks == cell_iota)[None], chosen.reshape(components, cell_rows, -1), 0.0)
        gain = face_gain_ref[pl.ds(side, 1), :]
        face_out[side, 0:components] = jnp.sum(here, axis=1) * gain
        face_out[side, components:ROWS] = jnp.zeros((ROWS - components, FACE_STEP), f32)
        return carry

    lax.fori_loop(0, 4, gather_faces, 0)
    pl.semaphore_wait(barrier, len(AROUND))
    sides = [(-1, 0, 1), (1, 0, 0), (0, -1, 3), (0, 1, 2)]
    face_copies = [
        pltpu.make_async_remote_copy(
            src_ref=face_out.at[d],
            dst_ref=face_in.at[opposite],
            send_sem=face_send.at[d],
            recv_sem=face_recv.at[opposite],
            device_id=at(da, dc),
            device_id_type=pl.DeviceIdType.MESH,
        )
        for d, (da, dc, opposite) in enumerate(sides)
    ]
    for copy in face_copies:
        copy.start()

    for load in loads[3:8]:
        load.wait()
    binned_ref[...] = jnp.zeros_like(binned_ref)

    def pellet_code(first):
        owner = owner_ref[0:1, pl.ds(first, POINT_STEP)]
        slot = slot_ref[0:1, pl.ds(first, POINT_STEP)]
        return owner // 2, one_hot((owner % 2) * PEL + slot, 2 * PEL)

    def interpolate(step, carry):
        first = pl.multiple_of(step * POINT_STEP, POINT_STEP)
        table = one_hot(block_ref[0:1, pl.ds(first, POINT_STEP)], blocks)
        picked = dot(split_ref[0:R * cell_rows], table).reshape(R, cell_rows, POINT_STEP)
        weights = weight_ref[:, pl.ds(first, POINT_STEP)].astype(f32)
        values = jnp.sum(picked * weights[None], axis=1)
        area = area_ref[0:1, pl.ds(first, POINT_STEP)]
        stacked = jnp.concatenate(
            [values * area, area, jnp.zeros((ROWS - R - 1, POINT_STEP), f32)], axis=0
        )
        high, low = split(stacked)
        pair, pellets = pellet_code(first)
        both = jnp.concatenate([high.astype(f32), low.astype(f32)], axis=0)
        masked = jnp.concatenate([jnp.where(pair == g, both, 0.0) for g in range(OWNER_PAIRS)], axis=0)
        binned_ref[...] += dot_t(masked.astype(bf16), pellets)
        return carry

    lax.fori_loop(0, points // POINT_STEP, interpolate, 0)
    for n in range(9):
        first = (n // 2) * 2 * ROWS
        lanes = slice((n % 2) * PEL, (n % 2 + 1) * PEL)
        part_out[n] = (
            binned_ref[first:first + ROWS, lanes] + binned_ref[first + ROWS:first + 2 * ROWS, lanes]
        )
    part_copies = [
        pltpu.make_async_remote_copy(
            src_ref=part_out.at[n],
            dst_ref=part_in.at[n],
            send_sem=part_send.at[n],
            recv_sem=part_recv.at[n],
            device_id=at(OFFSETS[n][0] - 1, OFFSETS[n][1] - 1),
            device_id_type=pl.DeviceIdType.MESH,
        )
        for n in AROUND
    ]
    for copy in part_copies:
        copy.start()

    for load in loads[8:]:
        load.wait()
    groups = blocks // GROUP
    width = components * GROUP

    for k in range(slots):
        table = one_hot(links_ref[k], blocks)
        coupled = dot(split_ref[0:rows], table).astype(bf16).reshape(components, cell_rows, blocks)
        for g in range(groups):
            lanes = slice(g * GROUP, (g + 1) * GROUP)
            coupled_ref[g, k * cell_rows:(k + 1) * cell_rows, 0:width] = jnp.concatenate(
                [coupled[q, :, lanes] for q in range(components)], axis=1
            )

    step = cell_rows // (points // POINT_STEP)
    mask = (
        lax.broadcasted_iota(jnp.int32, (1, GROUP, width), 2) % GROUP
        == lax.broadcasted_iota(jnp.int32, (1, GROUP, width), 1)
    )

    def couple(which, carry):
        first = pl.multiple_of(which * step, step)
        turned = [
            jnp.transpose(flux_ref[:, first + n].reshape(slots * cell_rows, blocks)) for n in range(step)
        ]
        for g in range(groups):
            left = jnp.concatenate([t[g * GROUP:(g + 1) * GROUP] for t in turned], axis=0)
            product = dot(left, coupled_ref[g, :, 0:width]).reshape(step, GROUP, width)
            grouped_ref[g, pl.ds(first, step), 0:width] = jnp.sum(jnp.where(mask, product, 0.0), axis=1)
        return carry


    totals = part_out[4]
    for copy in part_copies:
        copy.wait()
    for n in AROUND:
        totals = totals + part_in[n]
    mean = totals[0:R] / totals[R:R + 1]
    gain = jnp.concatenate([gain_ref[r] for r in range(R)], axis=0)
    rates = gain * mean / jnp.sqrt(1.0 + mean * mean)
    for r in range(R):
        rates_ref[r] = rates[r:r + 1]
    rate_out[0:R] = rates
    rate_out[R:ROWS] = jnp.zeros((ROWS - R, PEL), f32)
    rate_copies = [
        pltpu.make_async_remote_copy(
            src_ref=rate_out,
            dst_ref=rate_in.at[n],
            send_sem=rate_send.at[n],
            recv_sem=rate_recv.at[n],
            device_id=at(1 - OFFSETS[n][0], 1 - OFFSETS[n][1]),
            device_id_type=pl.DeviceIdType.MESH,
        )
        for n in AROUND
    ]
    for copy in rate_copies:
        copy.start()

    total_ref[...] = jnp.zeros_like(total_ref)
    for copy in face_copies:
        copy.wait()
    inside = [s > 0, s < stream_count - 1, x > 0, x < cross_count - 1]
    present = [jnp.where(here, 1.0, 0.0) for here in inside]
    for d in range(4):
        face_in[d] = face_in[d] * present[d] - face_out[d]

    def add_faces(side, carry):
        ids = cells_ref[pl.ds(side, 1), :]
        table = one_hot(ids % blocks, blocks)
        here = ids // blocks == cell_iota
        net = face_in[side, 0:components]
        spread = jnp.where(here[None], net[:, None, :], 0.0).reshape(rows, FACE_STEP)
        high, low = split(spread)
        total_ref[...] += dot_t(high, table) + dot_t(low, table)
        return carry

    lax.fori_loop(0, 4, add_faces, 0)

    rate_in[4] = rate_out[...]
    for copy in rate_copies:
        copy.wait()
    last_ref[...] = jnp.zeros_like(last_ref)
    for n in range(9):
        last_ref[n:n + 1] = rate_in[n, R - 1:R]
    code = lax.broadcasted_iota(jnp.int32, (ROWS, PEL), 0)

    def look_up(first):
        owner = jnp.broadcast_to(owner_ref[0:1, pl.ds(first, PEL)], (8, PEL))
        slot = jnp.broadcast_to(slot_ref[0:1, pl.ds(first, PEL)], (8, PEL))
        found = jnp.zeros((8, PEL), f32)
        for n in range(9):
            found = jnp.where(owner == n, jnp.take_along_axis(rate_in[n, 0:8], slot, axis=1), found)
        last = jnp.where(owner == code[0:8], jnp.take_along_axis(last_ref[0:8], slot, axis=1), 0.0)
        last = last + jnp.where(owner == code[8:ROWS], jnp.take_along_axis(last_ref[8:ROWS], slot, axis=1), 0.0)
        area = area_ref[0:1, pl.ds(first, PEL)]
        return found * area, jnp.sum(last, axis=0, keepdims=True) * area

    def deposit(which, carry):
        first = pl.multiple_of(which * POINT_STEP, POINT_STEP)
        for n in range(POINT_STEP // PEL):
            lanes = slice(n * PEL, (n + 1) * PEL)
            most, last = look_up(first + n * PEL)
            source_ref[0:8, lanes] = most
            source_ref[8:9, lanes] = last
        source = source_ref[...]
        table = one_hot(block_ref[0:1, pl.ds(first, POINT_STEP)], blocks)
        weights = weight_ref[:, pl.ds(first, POINT_STEP)].astype(f32)
        spread = (weights[None] * source[0:R, None, :]).astype(bf16).reshape(R * cell_rows, POINT_STEP)
        total_ref[0:R * cell_rows] += dot_t(spread, table)
        return couple(which, carry)

    lax.fori_loop(0, points // POINT_STEP, deposit, 0)
    for q in range(components):
        interior = jnp.concatenate(
            [grouped_ref[g, :, q * GROUP:(q + 1) * GROUP] for g in range(groups)], axis=1
        )
        added = total_ref[q * cell_rows:(q + 1) * cell_rows]
        next_ref[q] = state_ref[q] + phase_dt * (interior + added)


def shards(mesh_shape, *arrays):
    arrays = [array[0, 0] for array in arrays]
    (state, flux, links, cells, face_gain, owner, slot, block, weight, area, gain) = arrays
    components, cell_rows, blocks = state.shape
    slots = flux.shape[0]
    rows = components * cell_rows
    links = links[:, None]
    gain = gain[:, None]
    owner, slot, block, area = (a.reshape(1, -1) for a in (owner, slot, block, area))
    operands = (state, flux, links, cells, face_gain, owner, slot, block, weight, area, gain)
    faces = cells.shape[1]
    groups = blocks // GROUP
    dma = pltpu.SemaphoreType.DMA
    result, rates = pl.pallas_call(
        functools.partial(kernel, *mesh_shape),
        out_shape=(
            jax.ShapeDtypeStruct(state.shape, f32),
            jax.ShapeDtypeStruct(gain.shape, f32),
        ),
        in_specs=[pl.BlockSpec(memory_space=pl.ANY)] * len(operands),
        out_specs=(pl.BlockSpec(memory_space=pltpu.VMEM),) * 2,
        scratch_shapes=[pltpu.VMEM(a.shape, a.dtype) for a in operands]
        + [
            pltpu.VMEM((2 * rows, blocks), bf16),
            pltpu.VMEM((groups, slots * cell_rows, 256), bf16),
            pltpu.VMEM((groups, cell_rows, 256), f32),
            pltpu.VMEM((rows, blocks), f32),
            pltpu.VMEM((4, ROWS, faces), f32),
            pltpu.VMEM((4, ROWS, faces), f32),
            pltpu.VMEM((9, ROWS, PEL), f32),
            pltpu.VMEM((9, ROWS, PEL), f32),
            pltpu.VMEM((ROWS, PEL), f32),
            pltpu.VMEM((9, ROWS, PEL), f32),
            pltpu.VMEM((OWNER_PAIRS * 2 * ROWS, 2 * PEL), f32),
            pltpu.VMEM((ROWS, PEL), f32),
            pltpu.VMEM((ROWS, POINT_STEP), f32),
            dma((len(operands),)),
            dma((4,)),
            dma((4,)),
            dma((9,)),
            dma((9,)),
            dma((9,)),
            dma((9,)),
        ],
        compiler_params=pltpu.CompilerParams(
            collective_id=0, has_side_effects=True, vmem_limit_bytes=60 * 2**20
        ),
        name="bed_phase",
    )(*operands)
    return result[None, None], rates[None, None, :, 0]


def solution(mesh):
    def spec(dims):
        return P("stream", "cross", *([None] * dims))

    return jax.shard_map(
        functools.partial(shards, (mesh.shape["stream"], mesh.shape["cross"])),
        mesh=mesh,
        in_specs=tuple(spec(d) for d in (3, 4, 2, 2, 2, 1, 1, 1, 2, 1, 2)),
        out_specs=(spec(3), spec(2)),
        check_vma=False,
    )
```

```python
import functools

import jax
import jax.numpy as jnp
from jax import lax
from jax.experimental import pallas as pl
from jax.experimental.pallas import tpu as pltpu
from jax.sharding import PartitionSpec as P

R = 9
PEL = 128
GROUP = 16
POINT_STEP = 4096
FACE_STEP = 1536
OWNER_PAIRS = 5
ROWS = 16
PARTS = 2

phase_dt = 0.5
f32 = jnp.float32
bf16 = jnp.bfloat16
OFFSETS = [(a, c) for a in range(3) for c in range(3)]
AROUND = [n for n in range(9) if n != 4]


def one_hot(row, count):
    ids = row.astype(f32).astype(bf16)
    iota = lax.broadcasted_iota(jnp.int32, (count, row.shape[1]), 0).astype(f32).astype(bf16)
    return jnp.where(iota == ids, bf16(1), bf16(0))


def split(values):
    high = values.astype(bf16)
    return high, (values - high.astype(f32)).astype(bf16)


def dot(a, b):
    return jnp.dot(a, b, preferred_element_type=f32)


def dot_t(a, b):
    return lax.dot_general(a, b, (((1,), (1,)), ((), ())), preferred_element_type=f32)


def swap_parts(arrays):
    arrays = list(arrays)
    lane = lax.broadcasted_iota(jnp.int32, arrays[0].shape, 1) // GROUP
    for far in (4, 2, 1):
        low = (lane & far).astype(f32).astype(arrays[0].dtype) == 0
        for n in range(8):
            if n & far == 0:
                a, b = arrays[n], arrays[n + far]
                arrays[n] = jnp.where(low, a, jnp.roll(b, far * GROUP, axis=1))
                arrays[n + far] = jnp.where(low, jnp.roll(a, -far * GROUP, axis=1), b)
    return arrays


def kernel(
    stream_count,
    cross_count,
    state_hbm, flux_hbm, links_hbm, cells_hbm, face_gain_hbm, owner_hbm, slot_hbm, block_hbm,
    weight_hbm, area_hbm, gain_hbm,
    change_ref, rates_ref,
    state_ref, flux_ref, links_ref, cells_ref, face_gain_ref, owner_ref, slot_ref, block_ref,
    weight_ref, area_ref, gain_ref,
    split_ref, coupled_ref, interior_ref, total_ref,
    face_out, face_in, part_out, part_in, rate_out, rate_in, binned_ref, last_ref, source_ref,
    in_sem, face_send, face_recv, part_send, part_recv, rate_send, rate_recv,
):
    s, x = lax.axis_index("stream"), lax.axis_index("cross")
    components, cell_rows, blocks = state_ref.shape
    rows = components * cell_rows
    slots = flux_ref.shape[0]
    points = block_ref.shape[1]
    faces = face_gain_ref.shape[1]

    def at(first, second):
        return (
            lax.rem(s + (first + stream_count), stream_count),
            lax.rem(x + (second + cross_count), cross_count),
        )

    pairs = [
        (state_hbm, state_ref), (cells_hbm, cells_ref), (face_gain_hbm, face_gain_ref),
        (block_hbm, block_ref), (owner_hbm, owner_ref), (slot_hbm, slot_ref), (area_hbm, area_ref),
        (weight_hbm, weight_ref), (links_hbm, links_ref), (gain_hbm, gain_ref), (flux_hbm, flux_ref),
    ]
    loads = [pltpu.make_async_copy(a, b, in_sem.at[n]) for n, (a, b) in enumerate(pairs)]
    for load in loads:
        load.start()
    barrier = pltpu.get_barrier_semaphore()
    for n in AROUND:
        a, c = OFFSETS[n]
        pl.semaphore_signal(
            barrier, inc=1, device_id=at(a - 1, c - 1), device_id_type=pl.DeviceIdType.MESH
        )

    for load in loads[:3]:
        load.wait()
    high, low = split(state_ref[...].reshape(rows, blocks))
    split_ref[0:rows] = high
    split_ref[rows:2 * rows] = low
    cell_iota = lax.broadcasted_iota(jnp.int32, (cell_rows, FACE_STEP), 0)

    def gather_faces(side, carry):
        ids = cells_ref[pl.ds(side, 1), :]
        table = one_hot(ids % blocks, blocks)
        both = dot(split_ref[...], table)
        chosen = both[:rows] + both[rows:]
        here = jnp.where((ids // blocks == cell_iota)[None], chosen.reshape(components, cell_rows, -1), 0.0)
        gain = face_gain_ref[pl.ds(side, 1), :]
        face_out[side, 0:components] = jnp.sum(here, axis=1) * gain
        face_out[side, components:ROWS] = jnp.zeros((ROWS - components, FACE_STEP), f32)
        return carry

    lax.fori_loop(0, 4, gather_faces, 0)
    pl.semaphore_wait(barrier, len(AROUND))
    sides = [(-1, 0, 1), (1, 0, 0), (0, -1, 3), (0, 1, 2)]
    face_copies = [
        pltpu.make_async_remote_copy(
            src_ref=face_out.at[d],
            dst_ref=face_in.at[opposite],
            send_sem=face_send.at[d],
            recv_sem=face_recv.at[opposite],
            device_id=at(da, dc),
            device_id_type=pl.DeviceIdType.MESH,
        )
        for d, (da, dc, opposite) in enumerate(sides)
    ]
    for copy in face_copies:
        copy.start()

    for load in loads[3:9]:
        load.wait()
    binned_ref[...] = jnp.zeros_like(binned_ref)

    def pellet_code(first):
        owner = owner_ref[0:1, pl.ds(first, POINT_STEP)]
        slot = slot_ref[0:1, pl.ds(first, POINT_STEP)]
        return owner // 2, one_hot((owner % 2) * PEL + slot, 2 * PEL)

    groups = blocks // GROUP
    width = 256

    def arrange(k):
        table = one_hot(links_ref[k], blocks)
        coupled = dot(split_ref[0:rows], table).astype(bf16).reshape(components, cell_rows, blocks)
        place = pl.ds(pl.multiple_of(k * cell_rows, cell_rows), cell_rows)
        halves = [[coupled[q, :, h * 128:(h + 1) * 128] for q in range(components)] for h in range(2)]
        rest = swap_parts(halves[0][8:] + halves[1][8:])
        for h in range(2):
            for d, part in enumerate(swap_parts(halves[h][:8])):
                coupled_ref[h * 8 + d, place, 0:128] = part
                coupled_ref[h * 8 + d, place, 128:256] = rest[d]

    def interpolate(step, carry):
        first = pl.multiple_of(step * POINT_STEP, POINT_STEP)
        table = one_hot(block_ref[0:1, pl.ds(first, POINT_STEP)], blocks)
        picked = dot(split_ref[0:R * cell_rows], table).reshape(R, cell_rows, POINT_STEP)
        weights = weight_ref[:, pl.ds(first, POINT_STEP)].astype(f32)
        values = jnp.sum(picked * weights[None], axis=1)
        area = area_ref[0:1, pl.ds(first, POINT_STEP)]
        stacked = jnp.concatenate(
            [values * area, area, jnp.zeros((ROWS - R - 1, POINT_STEP), f32)], axis=0
        )
        high, low = split(stacked)
        pair, pellets = pellet_code(first)
        both = jnp.concatenate([high.astype(f32), low.astype(f32)], axis=0)
        masked = jnp.concatenate([jnp.where(pair == g, both, 0.0) for g in range(OWNER_PAIRS)], axis=0)
        binned_ref[...] += dot_t(masked.astype(bf16), pellets)
        arrange(jnp.minimum(step, slots - 1))
        return carry

    lax.fori_loop(0, points // POINT_STEP, interpolate, 0)
    for n in range(9):
        first = (n // 2) * 2 * ROWS
        lanes = slice((n % 2) * PEL, (n % 2 + 1) * PEL)
        part_out[n] = (
            binned_ref[first:first + ROWS, lanes] + binned_ref[first + ROWS:first + 2 * ROWS, lanes]
        )
    part_copies = [
        pltpu.make_async_remote_copy(
            src_ref=part_out.at[n],
            dst_ref=part_in.at[n],
            send_sem=part_send.at[n],
            recv_sem=part_recv.at[n],
            device_id=at(OFFSETS[n][0] - 1, OFFSETS[n][1] - 1),
            device_id_type=pl.DeviceIdType.MESH,
        )
        for n in AROUND
    ]
    for copy in part_copies:
        copy.start()

    for load in loads[9:]:
        load.wait()
    step = cell_rows // (points // POINT_STEP)
    mask = (
        lax.broadcasted_iota(jnp.int32, (1, GROUP, width), 2) % GROUP
        == lax.broadcasted_iota(jnp.int32, (1, GROUP, width), 1)
    )

    def couple(which, carry):
        first = pl.multiple_of(which * step, step)
        turned = [
            jnp.transpose(flux_ref[:, first + n].reshape(slots * cell_rows, blocks)) for n in range(step)
        ]
        found = []
        for g in range(groups):
            left = jnp.concatenate([t[g * GROUP:(g + 1) * GROUP] for t in turned], axis=0)
            product = dot(left, coupled_ref[g]).reshape(step, GROUP, width)
            found.append(jnp.sum(jnp.where(mask, product, 0.0), axis=1))
        for h in range(2):
            for q, part in enumerate(swap_parts([found[h * 8 + d][:, 0:128] for d in range(8)])):
                interior_ref[q, pl.ds(first, step), h * 128:(h + 1) * 128] = part
        front = lax.broadcasted_iota(jnp.int32, (step, 128), 1) < 64
        rest = [jnp.where(front, found[d][:, 128:256], found[8 + d][:, 128:256]) for d in range(8)]
        for n, part in enumerate(swap_parts(rest)):
            h = n // 4
            interior_ref[8 + n % 4, pl.ds(first, step), h * 128:(h + 1) * 128] = part
        return carry


    total_ref[...] = jnp.zeros_like(total_ref)
    for copy in face_copies:
        copy.wait()
    inside = [s > 0, s < stream_count - 1, x > 0, x < cross_count - 1]
    present = [jnp.where(here, 1.0, 0.0) for here in inside]
    for d in range(4):
        face_in[d] = face_in[d] * present[d] - face_out[d]

    def add_faces(side, carry):
        ids = cells_ref[pl.ds(side, 1), :]
        table = one_hot(ids % blocks, blocks)
        here = ids // blocks == cell_iota
        net = face_in[side, 0:components]
        spread = jnp.where(here[None], net[:, None, :], 0.0).reshape(rows, FACE_STEP)
        high, low = split(spread)
        total_ref[...] += dot_t(high, table) + dot_t(low, table)
        return carry

    lax.fori_loop(0, 2, add_faces, 0)

    totals = part_out[4]
    for copy in part_copies:
        copy.wait()
    for n in AROUND:
        totals = totals + part_in[n]
    mean = totals[0:R] / totals[R:R + 1]
    gain = jnp.concatenate([gain_ref[r] for r in range(R)], axis=0)
    rates = gain * mean / jnp.sqrt(1.0 + mean * mean)
    for r in range(R):
        rates_ref[r] = rates[r:r + 1]
    rate_out[0:R] = rates
    rate_out[R:ROWS] = jnp.zeros((ROWS - R, PEL), f32)
    rate_copies = [
        pltpu.make_async_remote_copy(
            src_ref=rate_out,
            dst_ref=rate_in.at[n],
            send_sem=rate_send.at[n],
            recv_sem=rate_recv.at[n],
            device_id=at(1 - OFFSETS[n][0], 1 - OFFSETS[n][1]),
            device_id_type=pl.DeviceIdType.MESH,
        )
        for n in AROUND
    ]
    for copy in rate_copies:
        copy.start()

    lax.fori_loop(2, 4, add_faces, 0)

    rate_in[4] = rate_out[...]
    for copy in rate_copies:
        copy.wait()
    last_ref[...] = jnp.zeros_like(last_ref)
    for n in range(9):
        last_ref[n:n + 1] = rate_in[n, R - 1:R]
    code = lax.broadcasted_iota(jnp.int32, (ROWS, PEL), 0)

    def look_up(first):
        owner = jnp.broadcast_to(owner_ref[0:1, pl.ds(first, PEL)], (8, PEL))
        slot = jnp.broadcast_to(slot_ref[0:1, pl.ds(first, PEL)], (8, PEL))
        found = jnp.zeros((8, PEL), f32)
        for n in range(9):
            found = jnp.where(owner == n, jnp.take_along_axis(rate_in[n, 0:8], slot, axis=1), found)
        last = jnp.where(owner == code[0:8], jnp.take_along_axis(last_ref[0:8], slot, axis=1), 0.0)
        last = last + jnp.where(owner == code[8:ROWS], jnp.take_along_axis(last_ref[8:ROWS], slot, axis=1), 0.0)
        area = area_ref[0:1, pl.ds(first, PEL)]
        return found * area, jnp.sum(last, axis=0, keepdims=True) * area

    def look_up_step(which, half):
        first = pl.multiple_of(which * POINT_STEP, POINT_STEP)
        for n in range(POINT_STEP // PEL):
            lanes = slice(n * PEL, (n + 1) * PEL)
            most, last = look_up(first + n * PEL)
            source_ref[half, 0:8, lanes] = most
            source_ref[half, 8:9, lanes] = last

    def deposit(which, carry):
        first = pl.multiple_of(which * POINT_STEP, POINT_STEP)
        source = source_ref[lax.rem(which, 2)]
        table = one_hot(block_ref[0:1, pl.ds(first, POINT_STEP)], blocks)
        weights = weight_ref[:, pl.ds(first, POINT_STEP)].astype(f32)
        spread = (weights[None] * source[0:R, None, :]).astype(bf16).reshape(R * cell_rows, POINT_STEP)
        total_ref[0:R * cell_rows] += dot_t(spread, table)
        couple(which, carry)
        look_up_step(jnp.minimum(which + 1, points // POINT_STEP - 1), lax.rem(which + 1, 2))
        return carry

    look_up_step(0, 0)
    lax.fori_loop(0, points // POINT_STEP, deposit, 0)
    for q in range(components):
        added = total_ref[q * cell_rows:(q + 1) * cell_rows]
        change_ref[q] = interior_ref[q] + added


def advance(state_ref, change_ref, found_ref, next_ref, rates_ref):
    next_ref[...] = state_ref[...] + phase_dt * change_ref[...]
    rates_ref[...] = found_ref[...]


def shards(mesh_shape, *arrays):
    arrays = [array[0, 0] for array in arrays]
    (state, flux, links, cells, face_gain, owner, slot, block, weight, area, gain) = arrays
    components, cell_rows, blocks = state.shape
    slots = flux.shape[0]
    rows = components * cell_rows
    links = links[:, None]
    gain = gain[:, None]
    owner, slot, block, area = (a.reshape(1, -1) for a in (owner, slot, block, area))
    operands = (state, flux, links, cells, face_gain, owner, slot, block, weight, area, gain)
    faces = cells.shape[1]
    groups = blocks // GROUP
    dma = pltpu.SemaphoreType.DMA
    change, found = pl.pallas_call(
        functools.partial(kernel, *mesh_shape),
        out_shape=(
            jax.ShapeDtypeStruct(state.shape, f32),
            jax.ShapeDtypeStruct(gain.shape, f32),
        ),
        in_specs=[pl.BlockSpec(memory_space=pl.ANY)] * len(operands),
        out_specs=(pl.BlockSpec(memory_space=pltpu.VMEM),) * 2,
        scratch_shapes=[pltpu.VMEM(a.shape, a.dtype) for a in operands]
        + [
            pltpu.VMEM((2 * rows, blocks), bf16),
            pltpu.VMEM((groups, slots * cell_rows, 256), bf16),
            pltpu.VMEM(state.shape, f32),
            pltpu.VMEM((rows, blocks), f32),
            pltpu.VMEM((4, ROWS, faces), f32),
            pltpu.VMEM((4, ROWS, faces), f32),
            pltpu.VMEM((9, ROWS, PEL), f32),
            pltpu.VMEM((9, ROWS, PEL), f32),
            pltpu.VMEM((ROWS, PEL), f32),
            pltpu.VMEM((9, ROWS, PEL), f32),
            pltpu.VMEM((OWNER_PAIRS * 2 * ROWS, 2 * PEL), f32),
            pltpu.VMEM((ROWS, PEL), f32),
            pltpu.VMEM((2, ROWS, POINT_STEP), f32),
            dma((len(operands),)),
            dma((4,)),
            dma((4,)),
            dma((9,)),
            dma((9,)),
            dma((9,)),
            dma((9,)),
        ],
        compiler_params=pltpu.CompilerParams(
            collective_id=0, has_side_effects=True, vmem_limit_bytes=60 * 2**20
        ),
        name="bed_phase",
    )(*operands)
    whole = pl.BlockSpec(gain.shape, lambda n: (0, 0, 0))
    part = pl.BlockSpec((components // PARTS,) + state.shape[1:], lambda n: (n, 0, 0))
    result, rates = pl.pallas_call(
        advance,
        grid=(PARTS,),
        out_shape=(
            jax.ShapeDtypeStruct(state.shape, f32),
            jax.ShapeDtypeStruct(gain.shape, f32),
        ),
        in_specs=[part, part, whole],
        out_specs=(part, whole),
        name="advance",
    )(state, change, found)
    return result[None, None], rates[None, None, :, 0]


def solution(mesh):
    def spec(dims):
        return P("stream", "cross", *([None] * dims))

    return jax.shard_map(
        functools.partial(shards, (mesh.shape["stream"], mesh.shape["cross"])),
        mesh=mesh,
        in_specs=tuple(spec(d) for d in (3, 4, 2, 2, 2, 1, 1, 1, 2, 1, 2)),
        out_specs=(spec(3), spec(2)),
        check_vma=False,
    )
```

```python
import functools

import jax
import jax.numpy as jnp
from jax import lax
from jax.experimental import pallas as pl
from jax.experimental.pallas import tpu as pltpu
from jax.sharding import PartitionSpec as P

R = 9
PEL = 128
GROUP = 16
POINT_STEP = 8192
FACE_STEP = 1536
OWNER_PAIRS = 5
ROWS = 16
PARTS = 2

phase_dt = 0.5
f32 = jnp.float32
bf16 = jnp.bfloat16
OFFSETS = [(a, c) for a in range(3) for c in range(3)]
AROUND = [n for n in range(9) if n != 4]


def one_hot(row, count):
    ids = row.astype(f32).astype(bf16)
    iota = lax.broadcasted_iota(jnp.int32, (count, row.shape[1]), 0).astype(f32).astype(bf16)
    return jnp.where(iota == ids, bf16(1), bf16(0))


def split(values):
    high = values.astype(bf16)
    return high, (values - high.astype(f32)).astype(bf16)


def dot(a, b):
    return jnp.dot(a, b, preferred_element_type=f32)


def dot_t(a, b):
    return lax.dot_general(a, b, (((1,), (1,)), ((), ())), preferred_element_type=f32)


def swap_parts(arrays):
    arrays = list(arrays)
    lane = lax.broadcasted_iota(jnp.int32, arrays[0].shape, 1) // GROUP
    for far in (4, 2, 1):
        low = (lane & far).astype(f32).astype(arrays[0].dtype) == 0
        for n in range(8):
            if n & far == 0:
                a, b = arrays[n], arrays[n + far]
                arrays[n] = jnp.where(low, a, jnp.roll(b, far * GROUP, axis=1))
                arrays[n + far] = jnp.where(low, jnp.roll(a, -far * GROUP, axis=1), b)
    return arrays


def kernel(
    stream_count,
    cross_count,
    state_hbm, flux_hbm, links_hbm, cells_hbm, face_gain_hbm, owner_hbm, slot_hbm, block_hbm,
    weight_hbm, area_hbm, gain_hbm,
    change_ref, rates_ref,
    state_ref, flux_ref, links_ref, cells_ref, face_gain_ref, owner_ref, slot_ref, block_ref,
    weight_ref, area_ref, gain_ref,
    split_ref, coupled_ref, interior_ref, total_ref,
    face_out, face_in, part_out, part_in, rate_out, rate_in, binned_ref, last_ref, source_ref,
    in_sem, face_send, face_recv, part_send, part_recv, rate_send, rate_recv,
):
    s, x = lax.axis_index("stream"), lax.axis_index("cross")
    components, cell_rows, blocks = state_ref.shape
    rows = components * cell_rows
    slots = flux_ref.shape[0]
    points = block_ref.shape[1]
    faces = face_gain_ref.shape[1]

    def at(first, second):
        return (
            lax.rem(s + (first + stream_count), stream_count),
            lax.rem(x + (second + cross_count), cross_count),
        )

    pairs = [
        (state_hbm, state_ref), (cells_hbm, cells_ref), (face_gain_hbm, face_gain_ref),
        (block_hbm, block_ref), (owner_hbm, owner_ref), (slot_hbm, slot_ref), (area_hbm, area_ref),
        (weight_hbm, weight_ref), (links_hbm, links_ref), (gain_hbm, gain_ref), (flux_hbm, flux_ref),
    ]
    loads = [pltpu.make_async_copy(a, b, in_sem.at[n]) for n, (a, b) in enumerate(pairs)]
    for load in loads:
        load.start()
    barrier = pltpu.get_barrier_semaphore()
    for n in AROUND:
        a, c = OFFSETS[n]
        pl.semaphore_signal(
            barrier, inc=1, device_id=at(a - 1, c - 1), device_id_type=pl.DeviceIdType.MESH
        )

    for load in loads[:3]:
        load.wait()
    high, low = split(state_ref[...].reshape(rows, blocks))
    split_ref[0:rows] = high
    split_ref[rows:2 * rows] = low
    cell_iota = lax.broadcasted_iota(jnp.int32, (cell_rows, FACE_STEP), 0)

    def gather_faces(side, carry):
        ids = cells_ref[pl.ds(side, 1), :]
        table = one_hot(ids % blocks, blocks)
        both = dot(split_ref[...], table)
        chosen = both[:rows] + both[rows:]
        here = jnp.where((ids // blocks == cell_iota)[None], chosen.reshape(components, cell_rows, -1), 0.0)
        gain = face_gain_ref[pl.ds(side, 1), :]
        face_out[side, 0:components] = jnp.sum(here, axis=1) * gain
        face_out[side, components:ROWS] = jnp.zeros((ROWS - components, FACE_STEP), f32)
        return carry

    lax.fori_loop(0, 4, gather_faces, 0)
    pl.semaphore_wait(barrier, len(AROUND))
    sides = [(-1, 0, 1), (1, 0, 0), (0, -1, 3), (0, 1, 2)]
    face_copies = [
        pltpu.make_async_remote_copy(
            src_ref=face_out.at[d],
            dst_ref=face_in.at[opposite],
            send_sem=face_send.at[d],
            recv_sem=face_recv.at[opposite],
            device_id=at(da, dc),
            device_id_type=pl.DeviceIdType.MESH,
        )
        for d, (da, dc, opposite) in enumerate(sides)
    ]
    for copy in face_copies:
        copy.start()

    for load in loads[3:9]:
        load.wait()
    binned_ref[...] = jnp.zeros_like(binned_ref)

    def pellet_code(first):
        owner = owner_ref[0:1, pl.ds(first, POINT_STEP)]
        slot = slot_ref[0:1, pl.ds(first, POINT_STEP)]
        return owner // 2, one_hot((owner % 2) * PEL + slot, 2 * PEL)

    groups = blocks // GROUP
    width = 256

    def arrange(k):
        table = one_hot(links_ref[k], blocks)
        coupled = dot(split_ref[0:rows], table).astype(bf16).reshape(components, cell_rows, blocks)
        place = pl.ds(pl.multiple_of(k * cell_rows, cell_rows), cell_rows)
        halves = [[coupled[q, :, h * 128:(h + 1) * 128] for q in range(components)] for h in range(2)]
        rest = swap_parts(halves[0][8:] + halves[1][8:])
        for h in range(2):
            for d, part in enumerate(swap_parts(halves[h][:8])):
                coupled_ref[h * 8 + d, place, 0:128] = part
                coupled_ref[h * 8 + d, place, 128:256] = rest[d]

    def interpolate(step, carry):
        first = pl.multiple_of(step * POINT_STEP, POINT_STEP)
        table = one_hot(block_ref[0:1, pl.ds(first, POINT_STEP)], blocks)
        picked = dot(split_ref[0:R * cell_rows], table).reshape(R, cell_rows, POINT_STEP)
        weights = weight_ref[:, pl.ds(first, POINT_STEP)].astype(f32)
        values = jnp.sum(picked * weights[None], axis=1)
        area = area_ref[0:1, pl.ds(first, POINT_STEP)]
        stacked = jnp.concatenate(
            [values * area, area, jnp.zeros((ROWS - R - 1, POINT_STEP), f32)], axis=0
        )
        high, low = split(stacked)
        pair, pellets = pellet_code(first)
        both = jnp.concatenate([high.astype(f32), low.astype(f32)], axis=0)
        masked = jnp.concatenate([jnp.where(pair == g, both, 0.0) for g in range(OWNER_PAIRS)], axis=0)
        binned_ref[...] += dot_t(masked.astype(bf16), pellets)
        for n in range(2):
            arrange(jnp.minimum(2 * step + n, slots - 1))
        return carry

    lax.fori_loop(0, points // POINT_STEP, interpolate, 0)
    for n in range(9):
        first = (n // 2) * 2 * ROWS
        lanes = slice((n % 2) * PEL, (n % 2 + 1) * PEL)
        part_out[n] = (
            binned_ref[first:first + ROWS, lanes] + binned_ref[first + ROWS:first + 2 * ROWS, lanes]
        )
    part_copies = [
        pltpu.make_async_remote_copy(
            src_ref=part_out.at[n],
            dst_ref=part_in.at[n],
            send_sem=part_send.at[n],
            recv_sem=part_recv.at[n],
            device_id=at(OFFSETS[n][0] - 1, OFFSETS[n][1] - 1),
            device_id_type=pl.DeviceIdType.MESH,
        )
        for n in AROUND
    ]
    for copy in part_copies:
        copy.start()

    for load in loads[9:]:
        load.wait()
    step = cell_rows // (points // POINT_STEP)
    mask = (
        lax.broadcasted_iota(jnp.int32, (1, GROUP, width), 2) % GROUP
        == lax.broadcasted_iota(jnp.int32, (1, GROUP, width), 1)
    )

    def couple(which, carry):
        first = pl.multiple_of(which * step, step)
        turned = [
            jnp.transpose(flux_ref[:, first + n].reshape(slots * cell_rows, blocks)) for n in range(step)
        ]
        found = []
        for g in range(groups):
            left = jnp.concatenate([t[g * GROUP:(g + 1) * GROUP] for t in turned], axis=0)
            product = dot(left, coupled_ref[g]).reshape(step, GROUP, width)
            found.append(jnp.sum(jnp.where(mask, product, 0.0), axis=1))
        for h in range(2):
            for q, part in enumerate(swap_parts([found[h * 8 + d][:, 0:128] for d in range(8)])):
                interior_ref[q, pl.ds(first, step), h * 128:(h + 1) * 128] = part
        front = lax.broadcasted_iota(jnp.int32, (step, 128), 1) < 64
        rest = [jnp.where(front, found[d][:, 128:256], found[8 + d][:, 128:256]) for d in range(8)]
        for n, part in enumerate(swap_parts(rest)):
            h = n // 4
            interior_ref[8 + n % 4, pl.ds(first, step), h * 128:(h + 1) * 128] = part
        return carry


    total_ref[...] = jnp.zeros_like(total_ref)
    for copy in face_copies:
        copy.wait()
    inside = [s > 0, s < stream_count - 1, x > 0, x < cross_count - 1]
    present = [jnp.where(here, 1.0, 0.0) for here in inside]
    for d in range(4):
        face_in[d] = face_in[d] * present[d] - face_out[d]

    def add_faces(side, carry):
        ids = cells_ref[pl.ds(side, 1), :]
        table = one_hot(ids % blocks, blocks)
        here = ids // blocks == cell_iota
        net = face_in[side, 0:components]
        spread = jnp.where(here[None], net[:, None, :], 0.0).reshape(rows, FACE_STEP)
        high, low = split(spread)
        total_ref[...] += dot_t(high, table) + dot_t(low, table)
        return carry

    lax.fori_loop(0, 2, add_faces, 0)

    totals = part_out[4]
    for copy in part_copies:
        copy.wait()
    for n in AROUND:
        totals = totals + part_in[n]
    mean = totals[0:R] / totals[R:R + 1]
    gain = jnp.concatenate([gain_ref[r] for r in range(R)], axis=0)
    rates = gain * mean / jnp.sqrt(1.0 + mean * mean)
    for r in range(R):
        rates_ref[r] = rates[r:r + 1]
    rate_out[0:R] = rates
    rate_out[R:ROWS] = jnp.zeros((ROWS - R, PEL), f32)
    rate_copies = [
        pltpu.make_async_remote_copy(
            src_ref=rate_out,
            dst_ref=rate_in.at[n],
            send_sem=rate_send.at[n],
            recv_sem=rate_recv.at[n],
            device_id=at(1 - OFFSETS[n][0], 1 - OFFSETS[n][1]),
            device_id_type=pl.DeviceIdType.MESH,
        )
        for n in AROUND
    ]
    for copy in rate_copies:
        copy.start()

    lax.fori_loop(2, 4, add_faces, 0)

    rate_in[4] = rate_out[...]
    for copy in rate_copies:
        copy.wait()
    last_ref[...] = jnp.zeros_like(last_ref)
    for n in range(9):
        last_ref[n:n + 1] = rate_in[n, R - 1:R]
    code = lax.broadcasted_iota(jnp.int32, (ROWS, PEL), 0)

    def look_up(first):
        owner = jnp.broadcast_to(owner_ref[0:1, pl.ds(first, PEL)], (8, PEL))
        slot = jnp.broadcast_to(slot_ref[0:1, pl.ds(first, PEL)], (8, PEL))
        found = jnp.zeros((8, PEL), f32)
        for n in range(9):
            found = jnp.where(owner == n, jnp.take_along_axis(rate_in[n, 0:8], slot, axis=1), found)
        last = jnp.where(owner == code[0:8], jnp.take_along_axis(last_ref[0:8], slot, axis=1), 0.0)
        last = last + jnp.where(owner == code[8:ROWS], jnp.take_along_axis(last_ref[8:ROWS], slot, axis=1), 0.0)
        area = area_ref[0:1, pl.ds(first, PEL)]
        return found * area, jnp.sum(last, axis=0, keepdims=True) * area

    def look_up_step(which, half):
        first = pl.multiple_of(which * POINT_STEP, POINT_STEP)
        for n in range(POINT_STEP // PEL):
            lanes = slice(n * PEL, (n + 1) * PEL)
            most, last = look_up(first + n * PEL)
            source_ref[half, 0:8, lanes] = most
            source_ref[half, 8:9, lanes] = last

    def deposit(which, carry):
        first = pl.multiple_of(which * POINT_STEP, POINT_STEP)
        source = source_ref[lax.rem(which, 2)]
        table = one_hot(block_ref[0:1, pl.ds(first, POINT_STEP)], blocks)
        weights = weight_ref[:, pl.ds(first, POINT_STEP)].astype(f32)
        spread = (weights[None] * source[0:R, None, :]).astype(bf16).reshape(R * cell_rows, POINT_STEP)
        total_ref[0:R * cell_rows] += dot_t(spread, table)
        couple(which, carry)
        look_up_step(jnp.minimum(which + 1, points // POINT_STEP - 1), lax.rem(which + 1, 2))
        return carry

    look_up_step(0, 0)
    lax.fori_loop(0, points // POINT_STEP, deposit, 0)
    for q in range(components):
        added = total_ref[q * cell_rows:(q + 1) * cell_rows]
        change_ref[q] = interior_ref[q] + added


def advance(state_ref, change_ref, found_ref, next_ref, rates_ref):
    next_ref[...] = state_ref[...] + phase_dt * change_ref[...]
    rates_ref[...] = found_ref[...]


def shards(mesh_shape, *arrays):
    arrays = [array[0, 0] for array in arrays]
    (state, flux, links, cells, face_gain, owner, slot, block, weight, area, gain) = arrays
    components, cell_rows, blocks = state.shape
    slots = flux.shape[0]
    rows = components * cell_rows
    links = links[:, None]
    gain = gain[:, None]
    owner, slot, block, area = (a.reshape(1, -1) for a in (owner, slot, block, area))
    operands = (state, flux, links, cells, face_gain, owner, slot, block, weight, area, gain)
    faces = cells.shape[1]
    groups = blocks // GROUP
    dma = pltpu.SemaphoreType.DMA
    change, found = pl.pallas_call(
        functools.partial(kernel, *mesh_shape),
        out_shape=(
            jax.ShapeDtypeStruct(state.shape, f32),
            jax.ShapeDtypeStruct(gain.shape, f32),
        ),
        in_specs=[pl.BlockSpec(memory_space=pl.ANY)] * len(operands),
        out_specs=(pl.BlockSpec(memory_space=pltpu.VMEM),) * 2,
        scratch_shapes=[pltpu.VMEM(a.shape, a.dtype) for a in operands]
        + [
            pltpu.VMEM((2 * rows, blocks), bf16),
            pltpu.VMEM((groups, slots * cell_rows, 256), bf16),
            pltpu.VMEM(state.shape, f32),
            pltpu.VMEM((rows, blocks), f32),
            pltpu.VMEM((4, ROWS, faces), f32),
            pltpu.VMEM((4, ROWS, faces), f32),
            pltpu.VMEM((9, ROWS, PEL), f32),
            pltpu.VMEM((9, ROWS, PEL), f32),
            pltpu.VMEM((ROWS, PEL), f32),
            pltpu.VMEM((9, ROWS, PEL), f32),
            pltpu.VMEM((OWNER_PAIRS * 2 * ROWS, 2 * PEL), f32),
            pltpu.VMEM((ROWS, PEL), f32),
            pltpu.VMEM((2, ROWS, POINT_STEP), f32),
            dma((len(operands),)),
            dma((4,)),
            dma((4,)),
            dma((9,)),
            dma((9,)),
            dma((9,)),
            dma((9,)),
        ],
        compiler_params=pltpu.CompilerParams(
            collective_id=0, has_side_effects=True, vmem_limit_bytes=60 * 2**20
        ),
        name="bed_phase",
    )(*operands)
    whole = pl.BlockSpec(gain.shape, lambda n: (0, 0, 0))
    part = pl.BlockSpec((components // PARTS,) + state.shape[1:], lambda n: (n, 0, 0))
    result, rates = pl.pallas_call(
        advance,
        grid=(PARTS,),
        out_shape=(
            jax.ShapeDtypeStruct(state.shape, f32),
            jax.ShapeDtypeStruct(gain.shape, f32),
        ),
        in_specs=[part, part, whole],
        out_specs=(part, whole),
        name="advance",
    )(state, change, found)
    return result[None, None], rates[None, None, :, 0]


def solution(mesh):
    def spec(dims):
        return P("stream", "cross", *([None] * dims))

    return jax.shard_map(
        functools.partial(shards, (mesh.shape["stream"], mesh.shape["cross"])),
        mesh=mesh,
        in_specs=tuple(spec(d) for d in (3, 4, 2, 2, 2, 1, 1, 1, 2, 1, 2)),
        out_specs=(spec(3), spec(2)),
        check_vma=False,
    )
```

```python
import functools

import jax
import jax.numpy as jnp
from jax import lax
from jax.experimental import pallas as pl
from jax.experimental.pallas import tpu as pltpu
from jax.sharding import PartitionSpec as P

R = 9
PEL = 128
GROUP = 16
POINT_STEP = 8192
FACE_STEP = 1536
OWNER_PAIRS = 5
ROWS = 16
PARTS = 2

phase_dt = 0.5
f32 = jnp.float32
bf16 = jnp.bfloat16
OFFSETS = [(a, c) for a in range(3) for c in range(3)]
AROUND = [n for n in range(9) if n != 4]


def one_hot(row, count):
    ids = row.astype(f32).astype(bf16)
    iota = lax.broadcasted_iota(jnp.int32, (count, row.shape[1]), 0).astype(f32).astype(bf16)
    return jnp.where(iota == ids, bf16(1), bf16(0))


def split(values):
    high = values.astype(bf16)
    return high, (values - high.astype(f32)).astype(bf16)


def dot(a, b):
    return jnp.dot(a, b, preferred_element_type=f32)


def dot_t(a, b):
    return lax.dot_general(a, b, (((1,), (1,)), ((), ())), preferred_element_type=f32)


def swap_parts(arrays):
    arrays = list(arrays)
    lane = lax.broadcasted_iota(jnp.int32, arrays[0].shape, 1) // GROUP
    for far in (4, 2, 1):
        low = (lane & far).astype(f32).astype(arrays[0].dtype) == 0
        for n in range(8):
            if n & far == 0:
                a, b = arrays[n], arrays[n + far]
                arrays[n] = jnp.where(low, a, jnp.roll(b, far * GROUP, axis=1))
                arrays[n + far] = jnp.where(low, jnp.roll(a, -far * GROUP, axis=1), b)
    return arrays


def kernel(
    stream_count,
    cross_count,
    state_hbm, flux_hbm, links_hbm, cells_hbm, face_gain_hbm, owner_hbm, slot_hbm, block_hbm,
    weight_hbm, area_hbm, gain_hbm,
    change_ref, rates_ref,
    state_ref, flux_ref, links_ref, cells_ref, face_gain_ref, owner_ref, slot_ref, block_ref,
    weight_ref, area_ref, gain_ref,
    split_ref, coupled_ref, interior_ref, total_ref,
    face_out, face_in, part_out, part_in, rate_out, rate_in, binned_ref, last_ref, source_ref,
    in_sem, face_send, face_recv, part_send, part_recv, rate_send, rate_recv,
):
    s, x = lax.axis_index("stream"), lax.axis_index("cross")
    components, cell_rows, blocks = state_ref.shape
    rows = components * cell_rows
    slots = flux_ref.shape[0]
    points = block_ref.shape[1]
    faces = face_gain_ref.shape[1]

    def at(first, second):
        return (
            lax.rem(s + (first + stream_count), stream_count),
            lax.rem(x + (second + cross_count), cross_count),
        )

    pairs = [
        (state_hbm, state_ref), (cells_hbm, cells_ref), (face_gain_hbm, face_gain_ref),
        (block_hbm, block_ref), (owner_hbm, owner_ref), (slot_hbm, slot_ref), (area_hbm, area_ref),
        (weight_hbm, weight_ref), (links_hbm, links_ref), (gain_hbm, gain_ref), (flux_hbm, flux_ref),
    ]
    loads = [pltpu.make_async_copy(a, b, in_sem.at[n]) for n, (a, b) in enumerate(pairs)]
    for load in loads[:-1]:
        load.start()
    barrier = pltpu.get_barrier_semaphore()
    for n in AROUND:
        a, c = OFFSETS[n]
        pl.semaphore_signal(
            barrier, inc=1, device_id=at(a - 1, c - 1), device_id_type=pl.DeviceIdType.MESH
        )

    for load in loads[:3]:
        load.wait()
    high, low = split(state_ref[...].reshape(rows, blocks))
    split_ref[0:rows] = high
    split_ref[rows:2 * rows] = low
    cell_iota = lax.broadcasted_iota(jnp.int32, (cell_rows, FACE_STEP), 0)

    def gather_faces(side, carry):
        ids = cells_ref[pl.ds(side, 1), :]
        table = one_hot(ids % blocks, blocks)
        both = dot(split_ref[...], table)
        chosen = both[:rows] + both[rows:]
        here = jnp.where((ids // blocks == cell_iota)[None], chosen.reshape(components, cell_rows, -1), 0.0)
        gain = face_gain_ref[pl.ds(side, 1), :]
        face_out[side, 0:components] = jnp.sum(here, axis=1) * gain
        face_out[side, components:ROWS] = jnp.zeros((ROWS - components, FACE_STEP), f32)
        return carry

    lax.fori_loop(0, 4, gather_faces, 0)
    loads[-1].start()
    pl.semaphore_wait(barrier, len(AROUND))
    sides = [(-1, 0, 1), (1, 0, 0), (0, -1, 3), (0, 1, 2)]
    face_copies = [
        pltpu.make_async_remote_copy(
            src_ref=face_out.at[d],
            dst_ref=face_in.at[opposite],
            send_sem=face_send.at[d],
            recv_sem=face_recv.at[opposite],
            device_id=at(da, dc),
            device_id_type=pl.DeviceIdType.MESH,
        )
        for d, (da, dc, opposite) in enumerate(sides)
    ]
    for copy in face_copies:
        copy.start()

    for load in loads[3:9]:
        load.wait()
    binned_ref[...] = jnp.zeros_like(binned_ref)

    def pellet_code(first):
        owner = owner_ref[0:1, pl.ds(first, POINT_STEP)]
        slot = slot_ref[0:1, pl.ds(first, POINT_STEP)]
        return owner // 2, one_hot((owner % 2) * PEL + slot, 2 * PEL)

    groups = blocks // GROUP
    width = 256

    def arrange(k):
        table = one_hot(links_ref[k], blocks)
        coupled = dot(split_ref[0:rows], table).astype(bf16).reshape(components, cell_rows, blocks)
        place = pl.ds(pl.multiple_of(k * cell_rows, cell_rows), cell_rows)
        halves = [[coupled[q, :, h * 128:(h + 1) * 128] for q in range(components)] for h in range(2)]
        rest = swap_parts(halves[0][8:] + halves[1][8:])
        for h in range(2):
            for d, part in enumerate(swap_parts(halves[h][:8])):
                coupled_ref[h * 8 + d, place, 0:128] = part
                coupled_ref[h * 8 + d, place, 128:256] = rest[d]

    def interpolate(step, carry):
        first = pl.multiple_of(step * POINT_STEP, POINT_STEP)
        table = one_hot(block_ref[0:1, pl.ds(first, POINT_STEP)], blocks)
        picked = dot(split_ref[0:R * cell_rows], table).reshape(R, cell_rows, POINT_STEP)
        weights = weight_ref[:, pl.ds(first, POINT_STEP)].astype(f32)
        values = jnp.sum(picked * weights[None], axis=1)
        area = area_ref[0:1, pl.ds(first, POINT_STEP)]
        stacked = jnp.concatenate(
            [values * area, area, jnp.zeros((ROWS - R - 1, POINT_STEP), f32)], axis=0
        )
        high, low = split(stacked)
        pair, pellets = pellet_code(first)
        both = jnp.concatenate([high.astype(f32), low.astype(f32)], axis=0)
        masked = jnp.concatenate([jnp.where(pair == g, both, 0.0) for g in range(OWNER_PAIRS)], axis=0)
        binned_ref[...] += dot_t(masked.astype(bf16), pellets)
        for n in range(2):
            arrange(jnp.minimum(2 * step + n, slots - 1))
        return carry

    lax.fori_loop(0, points // POINT_STEP, interpolate, 0)
    for n in range(9):
        first = (n // 2) * 2 * ROWS
        lanes = slice((n % 2) * PEL, (n % 2 + 1) * PEL)
        part_out[n] = (
            binned_ref[first:first + ROWS, lanes] + binned_ref[first + ROWS:first + 2 * ROWS, lanes]
        )
    part_copies = [
        pltpu.make_async_remote_copy(
            src_ref=part_out.at[n],
            dst_ref=part_in.at[n],
            send_sem=part_send.at[n],
            recv_sem=part_recv.at[n],
            device_id=at(OFFSETS[n][0] - 1, OFFSETS[n][1] - 1),
            device_id_type=pl.DeviceIdType.MESH,
        )
        for n in AROUND
    ]
    for copy in part_copies:
        copy.start()

    for load in loads[9:]:
        load.wait()
    step = cell_rows // (points // POINT_STEP)
    lane = lax.broadcasted_iota(jnp.int32, (8, 128), 1)
    row = lax.broadcasted_iota(jnp.int32, (8, 128), 0)

    def diagonal(product):
        merged = None
        for n in range(8):
            top = product[n * GROUP:n * GROUP + 8]
            here = jnp.where(lane % GROUP < 8, top, product[n * GROUP + 8:(n + 1) * GROUP])
            if n == 0:
                merged = here
            else:
                merged = jnp.where(row == (lane + n) % 8, pltpu.roll(here, n, 0), merged)
        for far in (1, 2, 4):
            merged = jnp.where(lane & far == 0, merged, pltpu.roll(merged, 8 - far, 0))
        return merged

    def couple(which, carry):
        first = pl.multiple_of(which * step, step)
        turned = [
            jnp.transpose(flux_ref[:, first + n].reshape(slots * cell_rows, blocks)) for n in range(step)
        ]
        found = []
        for g in range(groups):
            left = jnp.concatenate([t[g * GROUP:(g + 1) * GROUP] for t in turned], axis=0)
            product = dot(left, coupled_ref[g])
            found.append([
                jnp.concatenate([
                    diagonal(product[n * GROUP:(n + 8) * GROUP, h * 128:(h + 1) * 128])
                    for n in range(0, step, 8)
                ], axis=0)
                for h in range(2)
            ])
        for h in range(2):
            for q, part in enumerate(swap_parts([found[h * 8 + d][0] for d in range(8)])):
                interior_ref[q, pl.ds(first, step), h * 128:(h + 1) * 128] = part
        front = lax.broadcasted_iota(jnp.int32, (step, 128), 1) < 64
        rest = [jnp.where(front, found[d][1], found[8 + d][1]) for d in range(8)]
        for n, part in enumerate(swap_parts(rest)):
            h = n // 4
            interior_ref[8 + n % 4, pl.ds(first, step), h * 128:(h + 1) * 128] = part
        return carry


    total_ref[...] = jnp.zeros_like(total_ref)
    for copy in face_copies:
        copy.wait()
    inside = [s > 0, s < stream_count - 1, x > 0, x < cross_count - 1]
    present = [jnp.where(here, 1.0, 0.0) for here in inside]
    for d in range(4):
        face_in[d] = face_in[d] * present[d] - face_out[d]

    def add_faces(side, carry):
        ids = cells_ref[pl.ds(side, 1), :]
        table = one_hot(ids % blocks, blocks)
        here = ids // blocks == cell_iota
        net = face_in[side, 0:components]
        spread = jnp.where(here[None], net[:, None, :], 0.0).reshape(rows, FACE_STEP)
        high, low = split(spread)
        total_ref[...] += dot_t(high, table) + dot_t(low, table)
        return carry

    lax.fori_loop(0, 2, add_faces, 0)

    totals = part_out[4]
    for copy in part_copies:
        copy.wait()
    for n in AROUND:
        totals = totals + part_in[n]
    mean = totals[0:R] / totals[R:R + 1]
    gain = jnp.concatenate([gain_ref[r] for r in range(R)], axis=0)
    rates = gain * mean / jnp.sqrt(1.0 + mean * mean)
    for r in range(R):
        rates_ref[r] = rates[r:r + 1]
    rate_out[0:R] = rates
    rate_out[R:ROWS] = jnp.zeros((ROWS - R, PEL), f32)
    rate_copies = [
        pltpu.make_async_remote_copy(
            src_ref=rate_out,
            dst_ref=rate_in.at[n],
            send_sem=rate_send.at[n],
            recv_sem=rate_recv.at[n],
            device_id=at(1 - OFFSETS[n][0], 1 - OFFSETS[n][1]),
            device_id_type=pl.DeviceIdType.MESH,
        )
        for n in AROUND
    ]
    for copy in rate_copies:
        copy.start()

    lax.fori_loop(2, 4, add_faces, 0)

    rate_in[4] = rate_out[...]
    for copy in rate_copies:
        copy.wait()
    last_ref[...] = jnp.zeros_like(last_ref)
    for n in range(9):
        last_ref[n:n + 1] = rate_in[n, R - 1:R]
    code = lax.broadcasted_iota(jnp.int32, (ROWS, PEL), 0)

    def look_up(first):
        owner = jnp.broadcast_to(owner_ref[0:1, pl.ds(first, PEL)], (8, PEL))
        slot = jnp.broadcast_to(slot_ref[0:1, pl.ds(first, PEL)], (8, PEL))
        found = jnp.zeros((8, PEL), f32)
        for n in range(9):
            found = jnp.where(owner == n, jnp.take_along_axis(rate_in[n, 0:8], slot, axis=1), found)
        last = jnp.where(owner == code[0:8], jnp.take_along_axis(last_ref[0:8], slot, axis=1), 0.0)
        last = last + jnp.where(owner == code[8:ROWS], jnp.take_along_axis(last_ref[8:ROWS], slot, axis=1), 0.0)
        area = area_ref[0:1, pl.ds(first, PEL)]
        return found * area, jnp.sum(last, axis=0, keepdims=True) * area

    def look_up_step(which, half):
        first = pl.multiple_of(which * POINT_STEP, POINT_STEP)
        for n in range(POINT_STEP // PEL):
            lanes = slice(n * PEL, (n + 1) * PEL)
            most, last = look_up(first + n * PEL)
            source_ref[half, 0:8, lanes] = most
            source_ref[half, 8:9, lanes] = last

    def deposit(which, carry):
        first = pl.multiple_of(which * POINT_STEP, POINT_STEP)
        source = source_ref[lax.rem(which, 2)]
        table = one_hot(block_ref[0:1, pl.ds(first, POINT_STEP)], blocks)
        weights = weight_ref[:, pl.ds(first, POINT_STEP)].astype(f32)
        spread = (weights[None] * source[0:R, None, :]).astype(bf16).reshape(R * cell_rows, POINT_STEP)
        total_ref[0:R * cell_rows] += dot_t(spread, table)
        couple(which, carry)
        look_up_step(jnp.minimum(which + 1, points // POINT_STEP - 1), lax.rem(which + 1, 2))
        return carry

    look_up_step(0, 0)
    lax.fori_loop(0, points // POINT_STEP, deposit, 0)
    for q in range(components):
        added = total_ref[q * cell_rows:(q + 1) * cell_rows]
        change_ref[q] = interior_ref[q] + added


def advance(state_ref, change_ref, found_ref, next_ref, rates_ref):
    next_ref[...] = state_ref[...] + phase_dt * change_ref[...]
    rates_ref[...] = found_ref[...]


def shards(mesh_shape, *arrays):
    arrays = [array[0, 0] for array in arrays]
    (state, flux, links, cells, face_gain, owner, slot, block, weight, area, gain) = arrays
    components, cell_rows, blocks = state.shape
    slots = flux.shape[0]
    rows = components * cell_rows
    links = links[:, None]
    gain = gain[:, None]
    owner, slot, block, area = (a.reshape(1, -1) for a in (owner, slot, block, area))
    operands = (state, flux, links, cells, face_gain, owner, slot, block, weight, area, gain)
    faces = cells.shape[1]
    groups = blocks // GROUP
    dma = pltpu.SemaphoreType.DMA
    change, found = pl.pallas_call(
        functools.partial(kernel, *mesh_shape),
        out_shape=(
            jax.ShapeDtypeStruct(state.shape, f32),
            jax.ShapeDtypeStruct(gain.shape, f32),
        ),
        in_specs=[pl.BlockSpec(memory_space=pl.ANY)] * len(operands),
        out_specs=(pl.BlockSpec(memory_space=pltpu.VMEM),) * 2,
        scratch_shapes=[pltpu.VMEM(a.shape, a.dtype) for a in operands]
        + [
            pltpu.VMEM((2 * rows, blocks), bf16),
            pltpu.VMEM((groups, slots * cell_rows, 256), bf16),
            pltpu.VMEM(state.shape, f32),
            pltpu.VMEM((rows, blocks), f32),
            pltpu.VMEM((4, ROWS, faces), f32),
            pltpu.VMEM((4, ROWS, faces), f32),
            pltpu.VMEM((9, ROWS, PEL), f32),
            pltpu.VMEM((9, ROWS, PEL), f32),
            pltpu.VMEM((ROWS, PEL), f32),
            pltpu.VMEM((9, ROWS, PEL), f32),
            pltpu.VMEM((OWNER_PAIRS * 2 * ROWS, 2 * PEL), f32),
            pltpu.VMEM((ROWS, PEL), f32),
            pltpu.VMEM((2, ROWS, POINT_STEP), f32),
            dma((len(operands),)),
            dma((4,)),
            dma((4,)),
            dma((9,)),
            dma((9,)),
            dma((9,)),
            dma((9,)),
        ],
        compiler_params=pltpu.CompilerParams(
            collective_id=0, has_side_effects=True, vmem_limit_bytes=60 * 2**20
        ),
        name="bed_phase",
    )(*operands)
    whole = pl.BlockSpec(gain.shape, lambda n: (0, 0, 0))
    part = pl.BlockSpec((components // PARTS,) + state.shape[1:], lambda n: (n, 0, 0))
    result, rates = pl.pallas_call(
        advance,
        grid=(PARTS,),
        out_shape=(
            jax.ShapeDtypeStruct(state.shape, f32),
            jax.ShapeDtypeStruct(gain.shape, f32),
        ),
        in_specs=[part, part, whole],
        out_specs=(part, whole),
        name="advance",
    )(state, change, found)
    return result[None, None], rates[None, None, :, 0]


def solution(mesh):
    def spec(dims):
        return P("stream", "cross", *([None] * dims))

    return jax.shard_map(
        functools.partial(shards, (mesh.shape["stream"], mesh.shape["cross"])),
        mesh=mesh,
        in_specs=tuple(spec(d) for d in (3, 4, 2, 2, 2, 1, 1, 1, 2, 1, 2)),
        out_specs=(spec(3), spec(2)),
        check_vma=False,
    )
```
